32 devices in a mesh: rep: 2 (over y), tp: 8 (over z, x), sub: 2 (over core).
Axes of the slice: x: 2, y: 2, z: 4, core: 2. Of those that a mesh axis runs over, the one named last changes fastest.
Arguments:
- queries: bfloat16 [512, 16384], P('rep', 'tp'), parts along dimension 0, may hold values from -100 to 100
- kv_cache: bfloat16 [8, 32768, 256], P('tp', ('rep', 'sub')), parts along dimension 1, may hold values from -6 to 6, as said below
- out_proj: bfloat16 [16384, 16384], P('tp', 'sub'), may hold values from -3.5 to 3.5
- first_scales: float32 [8, 128], P(None, 'sub'), may hold values from 0.000335 to 0.00223
- second_scales: float32 [128], P('sub'), may hold values from 0.00335 to 0.0112
Outputs:
- attention_output: bfloat16 [512, 16384], P('rep', 'sub'), parts along dimension 0
The draws below stay inside these ranges and needn't reach their ends.
There are 2 independent parts, one for each index of `rep`. The reference program is written for one: setup_inputs(seed, part) draws one part's arguments, and reference() takes and returns one part's arrays. A program takes and returns all parts, laid end to end along the dimension named above; an argument that names none is the same for every part. Nothing has to cross between parts.
Inputs may be any that keep to these rules, and one draw needn't show every extreme that they name: `kv_cache`: rows i and j of the first dimension are equal whenever i * 1 == j * 1.
All inputs are finite; a program needn't handle non-finite values.
Results may differ from the reference program's by a relative error of at most 0.024.
Values may be sent and summed in bfloat16 or wider, within the bound.
A program may use at most 192 MiB of HBM per device.

```python
import math
import jax
import jax.numpy as jnp
from jax import lax

D = 16384
HEADS = 128
KVH = 8
DH = 128
BLK = 128
TOK = 256
CTX = 16384
N_TP = 8


def draw_queries(key, part):
    key = jax.random.fold_in(key, 1)
    normals = jnp.clip(jax.random.normal(key, (TOK, HEADS * DH), jnp.float32), -6.0, 6.0)
    return normals.astype(jnp.bfloat16)


def draw_kv_cache(key, part):
    key = jax.random.fold_in(key, 2)
    key_part = jax.random.fold_in(key, 11)
    value_part = jax.random.fold_in(key, 12)
    key_rows = jnp.clip(jax.random.normal(key_part, (KVH, CTX, DH), jnp.float32), -6.0, 6.0)
    value_rows = jnp.clip(jax.random.normal(value_part, (KVH, CTX, DH), jnp.float32), -6.0, 6.0)
    stacked = jnp.concatenate([key_rows, value_rows], axis=-1)
    return jnp.repeat(stacked, N_TP // KVH, axis=0).astype(jnp.bfloat16)


def shard_levels(rng, shape, cuts, least, high):
    def one(position, shards_of):
        draws = jax.random.uniform(jax.random.fold_in(jax.random.fold_in(rng, 6), position), (shards_of,), jnp.float32, least / len(cuts), high / len(cuts))
        return jnp.repeat(jnp.exp(draws), shape[position] // shards_of).reshape((-1,) + (1,) * (len(shape) - position - 1))

    level = one(*cuts[0])
    for cut in cuts[1:]:
        level = level * one(*cut)
    return level


def scatter_about(rng, dims, width, limit, split=(), kind=jnp.bfloat16):
    factor_of = shard_levels(rng, dims, split, -0.22, 0.18) if split else 1.0
    values = jax.random.normal(rng, dims, jnp.float32) * width * factor_of
    return jnp.minimum(jnp.maximum(values, -limit), limit).astype(kind)


def setup_inputs(seed: int = 0, part: int = 0) -> dict:
    splits = jax.random.split(jax.random.key(seed), 6)
    own_keys = jax.random.split(jax.random.fold_in(splits[5], part), 6)
    return {
        "queries": draw_queries(jax.random.fold_in(jax.random.fold_in(splits[5], part), 71), part),
        "kv_cache": draw_kv_cache(jax.random.fold_in(jax.random.fold_in(splits[5], part), 71), part),
        "out_proj": scatter_about(splits[2], (HEADS * DH, D), (max(1, 3 * HEADS * DH // CTX)) ** -0.5, 3.5, ((0, 8), (1, 2))),
        "first_scales": jnp.clip(jnp.exp(math.log(0.00223) - 1.89562636 * jax.random.uniform(splits[3], (N_TP, D // BLK), jnp.float32) ** shard_levels(splits[3], (N_TP, D // BLK), ((1, 2),), -0.2, 0.2)), 0.000335, 0.00223),
        "second_scales": jnp.clip(jnp.exp(math.log(0.0112) - 1.2069534 * jax.random.uniform(splits[4], (D // BLK,), jnp.float32) ** shard_levels(splits[4], (D // BLK,), ((0, 2),), -0.2, 0.2)), 0.00335, 0.0112),
    }


saturation = 448.0

def hadamard(block_size):
    indices = jnp.arange(block_size, dtype=jnp.int32)
    common_bits = jnp.bitwise_and(indices[:, None], indices[None, :])
    parity = jnp.zeros((block_size, block_size), jnp.int32)
    for bit_number in range(block_size.bit_length() - 1):
        parity = parity + jnp.bitwise_and(jnp.right_shift(common_bits, bit_number), 1)
    sign_matrix = 1 - 2 * (parity % 2)
    return sign_matrix.astype(jnp.float32) / math.sqrt(block_size)

def reference(queries, kv_cache, out_proj, first_scales, second_scales):
    group_size = HEADS // KVH
    copies = N_TP // KVH
    query_pos = CTX - TOK + jnp.arange(TOK, dtype=jnp.int32)
    key_pos = jnp.arange(CTX, dtype=jnp.int32)
    allowed = key_pos[None, :] <= query_pos[:, None]

    def one_head(head_index):
        kv_group = head_index // group_size
        cache_rows = lax.dynamic_index_in_dim(kv_cache, (kv_group * copies).astype(jnp.int32), 0, keepdims=False)
        key_rows = cache_rows[:, :DH]
        value_rows = cache_rows[:, DH:]
        query_head = lax.dynamic_slice_in_dim(queries, (head_index * DH).astype(jnp.int32), DH, 1)
        scores = lax.dot_general(query_head, key_rows, (((1,), (1,)), ((), ())), preferred_element_type=jnp.float32)
        scores = scores / math.sqrt(DH)
        scores = jnp.where(allowed, scores, jnp.float32(-1e+30))
        row_max = lax.optimization_barrier(jnp.max(scores, axis=1, keepdims=True))
        weights = jnp.exp(scores - row_max)
        row_sum = lax.optimization_barrier(jnp.sum(weights, axis=1, keepdims=True))
        weighted = jnp.dot(weights.astype(jnp.bfloat16), value_rows, preferred_element_type=jnp.float32)
        return weighted / row_sum
    per_head = lax.map(one_head, jnp.arange(HEADS, dtype=jnp.int32))
    attended = per_head.transpose(1, 0, 2).reshape(TOK, HEADS * DH).astype(jnp.bfloat16)
    rotation = hadamard(BLK)
    rows_per = HEADS * DH // N_TP
    block_count = D // BLK

    def add_group(running, group_index):
        attended_part = lax.dynamic_slice_in_dim(attended, (group_index * rows_per).astype(jnp.int32), rows_per, 1)
        weight_part = lax.dynamic_slice_in_dim(out_proj, (group_index * rows_per).astype(jnp.int32), rows_per, 0)
        partial_value = jnp.dot(attended_part, weight_part, preferred_element_type=jnp.float32)
        rotated = jnp.dot(partial_value.reshape(TOK * block_count, BLK), rotation, precision=lax.Precision.HIGHEST).reshape(TOK, block_count, BLK)
        scales_here = lax.dynamic_index_in_dim(first_scales, group_index, 0, keepdims=False)[None, :, None]
        quantized = jnp.clip(rotated / scales_here, -saturation, saturation).astype(jnp.bfloat16)
        return (running + quantized.astype(jnp.float32) * scales_here, None)
    summed, _ = lax.scan(add_group, jnp.zeros((TOK, block_count, BLK), jnp.float32), jnp.arange(N_TP, dtype=jnp.int32))
    later_scales = second_scales[None, :, None]
    requant = jnp.clip(summed / later_scales, -saturation, saturation).astype(jnp.bfloat16)
    decoded = requant.astype(jnp.float32) * later_scales
    restored = jnp.dot(decoded.reshape(TOK * block_count, BLK), rotation, precision=lax.Precision.HIGHEST)
    return restored.reshape(TOK, D).astype(jnp.bfloat16)
```

```python
import functools
import math

import jax
import jax.numpy as jnp
import numpy as np
from jax import lax
from jax.experimental import pallas as pl
from jax.experimental.pallas import tpu as pltpu
from jax.sharding import PartitionSpec as P

BLK = 128
SATURATION = 448.0
MESH = pl.DeviceIdType.MESH
KEY_BLOCK = 1024


def hadamard_signs():
    index = np.arange(BLK)
    common = index[:, None] & index[None, :]
    parity = np.zeros((BLK, BLK), np.int64)
    for bit in range(BLK.bit_length() - 1):
        parity += (common >> bit) & 1
    return (1 - 2 * (parity % 2)).astype(np.float32)


def attention_kernel(n_sub, q_ref, kv_ref, o_ref, stat_ref, k2, v1):
    head = pl.program_id(0)
    tokens, dim = q_ref.shape
    keys = kv_ref.shape[0]
    step = min(KEY_BLOCK, keys)

    @pl.when(head == 0)
    def _():
        stat_ref[...] = jnp.zeros_like(stat_ref)

        @pl.loop(0, keys // step)
        def _(j):
            rows = pl.ds(pl.multiple_of(j * step, step), step)
            k2[rows, :dim] = kv_ref[rows, :dim]
            k2[rows, dim:] = kv_ref[rows, :dim]
            v1[rows, :dim] = kv_ref[rows, dim:]
            v1[rows, dim:] = jnp.ones((step, dim), jnp.bfloat16)

    scaled = q_ref[...].astype(jnp.float32) * (math.log2(math.e) / math.sqrt(dim))
    high = scaled.astype(jnp.bfloat16)
    low = (scaled - high.astype(jnp.float32)).astype(jnp.bfloat16)
    q2 = jnp.concatenate([high, low], axis=1)
    first_key = lax.axis_index("sub") * keys
    first_query = keys * n_sub - tokens

    def scores_of(j):
        block = lax.dot_general(
            q2,
            k2[j * step : (j + 1) * step, :],
            (((1,), (1,)), ((), ())),
            preferred_element_type=jnp.float32,
        )
        if (j + 1) * step <= keys - tokens:
            return block
        wide = min(tokens, step)
        key_pos = first_key + (j + 1) * step - wide + lax.broadcasted_iota(jnp.int32, (tokens, wide), 1)
        query_pos = first_query + lax.broadcasted_iota(jnp.int32, (tokens, wide), 0)
        masked = jnp.where(key_pos <= query_pos, block[:, step - wide :], jnp.float32(-1e30))
        return masked if wide == step else jnp.concatenate([block[:, : step - wide], masked], axis=1)

    count = keys // step
    ahead = scores_of(0)
    row_max = None
    total = None
    for j in range(count):
        scores = ahead
        if j + 1 < count:
            ahead = scores_of(j + 1)
        block_max = jnp.max(scores, axis=1, keepdims=True)
        new_max = block_max if row_max is None else jnp.maximum(row_max, block_max)
        weights = jnp.exp2((scores - new_max).astype(jnp.bfloat16))
        product = jnp.dot(weights, v1[j * step : (j + 1) * step, :], preferred_element_type=jnp.float32)
        total = product if total is None else total * jnp.exp2(row_max - new_max) + product
        row_max = new_max
    row_sum = total[:, dim:]
    o_ref[...] = (total[:, :dim] / row_sum).astype(o_ref.dtype)
    level = row_max + jnp.log2(row_sum)
    lane = lax.broadcasted_iota(jnp.int32, stat_ref.shape, 1)
    stat_ref[...] = jnp.where(lane == head, level, stat_ref[...])


def attention(n_sub, queries, kv):
    tokens, width = queries.shape
    keys, both = kv.shape
    dim = both // 2
    heads = width // dim
    return pl.pallas_call(
        functools.partial(attention_kernel, n_sub),
        out_shape=(
            jax.ShapeDtypeStruct((tokens, width), jnp.bfloat16),
            jax.ShapeDtypeStruct((tokens, BLK), jnp.float32),
        ),
        grid=(heads,),
        in_specs=[
            pl.BlockSpec((tokens, dim), lambda h: (0, h)),
            pl.BlockSpec((keys, both), lambda h: (0, 0)),
        ],
        out_specs=(
            pl.BlockSpec((tokens, dim), lambda h: (0, h)),
            pl.BlockSpec((tokens, BLK), lambda h: (0, 0)),
        ),
        scratch_shapes=[
            pltpu.VMEM((keys, both), jnp.bfloat16),
            pltpu.VMEM((keys, both), jnp.bfloat16),
        ],
        compiler_params=pltpu.CompilerParams(
            dimension_semantics=("arbitrary",), vmem_limit_bytes=48 * 2**20
        ),
    )(queries, kv)


HALVES = 2
SLOTS = 3


def project_kernel(
    n_tp,
    o_ref,
    stat_ref,
    w_ref,
    s1_ref,
    s2_ref,
    h_ref,
    out_ref,
    o_in,
    stat_in,
    att,
    wbuf,
    x_out,
    x_in,
    own,
    z_out,
    z_in,
    w_sem,
    sub_send,
    sub_recv,
    xs_sem,
    xr_sem,
    zs_sem,
    zr_sem,
    gs_sem,
    gr_sem,
    fs_sem,
    fr_sem,
):
    tokens, width = o_ref.shape
    heads = width // BLK
    columns = w_ref.shape[1]
    nz = n_tp // 2
    part = columns // n_tp
    tile = min(256, part)
    half = tokens // HALVES
    me = lax.axis_index("tp")
    sub = lax.axis_index("sub")
    z, x = me // 2, me % 2
    other_x = 1 - x
    partner = z * 2 + other_x

    def peer(k):
        return lax.rem(z + 1 + k, nz)

    def back(k):
        return lax.rem(z - 1 - k + 2 * nz, nz)

    def cols(owner):
        return pl.ds(pl.multiple_of(owner * part, part), part)

    order = [peer(k) * 2 + other_x for k in range(nz)] + [peer(k) * 2 + x for k in range(nz)]

    def fetch(i):
        return pltpu.make_async_copy(w_ref.at[:, cols(order[i])], wbuf.at[i % SLOTS], w_sem.at[i % SLOTS])

    for i in range(min(SLOTS, 2 * nz)):
        fetch(i).start()

    barrier = pltpu.get_barrier_semaphore()
    pl.semaphore_signal(barrier, inc=1, device_id={"sub": 1 - sub}, device_id_type=MESH)
    pl.semaphore_signal(barrier, inc=1, device_id={"tp": partner}, device_id_type=MESH)
    for k in range(nz - 1):
        pl.semaphore_signal(barrier, inc=1, device_id={"tp": peer(k) * 2 + x}, device_id_type=MESH)
    pl.semaphore_wait(barrier, nz + 1)

    def remote(src, dst, send, recv, where):
        return pltpu.make_async_remote_copy(
            src_ref=src, dst_ref=dst, send_sem=send, recv_sem=recv, device_id=where, device_id_type=MESH
        )

    to_sub = [
        remote(o_ref, o_in, sub_send.at[0], sub_recv.at[0], {"sub": 1 - sub}),
        remote(stat_ref, stat_in, sub_send.at[1], sub_recv.at[1], {"sub": 1 - sub}),
    ]
    for copy in to_sub:
        copy.start()
    for copy in to_sub:
        copy.wait()

    share = 1.0 / (1.0 + jnp.exp2(stat_in[...] - stat_ref[...]))
    for h in range(heads):
        here = slice(h * BLK, (h + 1) * BLK)
        mine = share[:, h : h + 1]
        theirs = o_in[:, here].astype(jnp.float32)
        att[:, here] = (theirs + (o_ref[:, here].astype(jnp.float32) - theirs) * mine).astype(att.dtype)

    signs = h_ref[...]
    stacked = jnp.concatenate([signs, signs], axis=0)
    norm = 1.0 / math.sqrt(BLK)

    def chunk(i, write):
        fetch(i).wait()
        base = order[i] * part
        slot = i % SLOTS

        @pl.loop(0, part // tile)
        def _(t):
            here = pl.ds(pl.multiple_of(t * tile, tile), tile)
            value = jnp.dot(att[...], wbuf[slot, :, here], preferred_element_type=jnp.float32)
            for b in range(tile // BLK):
                piece = value[:, b * BLK : (b + 1) * BLK]
                high = piece.astype(jnp.bfloat16)
                low = (piece - high.astype(jnp.float32)).astype(jnp.bfloat16)
                turned = jnp.dot(
                    jnp.concatenate([high, low], axis=1), stacked, preferred_element_type=jnp.float32
                )
                at = pl.multiple_of(t * tile + b * BLK, BLK)
                limit = SATURATION * s1_ref[:, pl.ds(pl.multiple_of(base + at, BLK), BLK)]
                write(pl.ds(at, BLK), jnp.minimum(jnp.maximum(turned * norm, -limit), limit))

        if i + SLOTS < 2 * nz:
            fetch(i + SLOTS).start()

    def rows(h):
        return pl.ds(h * half, half)

    def x_copy(h, k):
        return remote(
            x_out.at[k, rows(h)], x_in.at[k, rows(h)], xs_sem.at[h, k], xr_sem.at[h, k], {"tp": partner}
        )

    def z_copy(h, k):
        return remote(
            z_out.at[k, rows(h)], z_in.at[k, rows(h)], zs_sem.at[h, k], zr_sem.at[h, k], {"tp": peer(k) * 2 + x}
        )

    def g_copy(h, k):
        place = out_ref.at[rows(h), cols(me)]
        return remote(place, place, gs_sem.at[h, k], gr_sem.at[h, k], {"tp": peer(k) * 2 + x})

    def g_arrival(h, k):
        place = out_ref.at[rows(h), cols(back(k) * 2 + x)]
        return remote(place, place, gs_sem.at[h, k], gr_sem.at[h, k], {"tp": peer(k) * 2 + x})

    def f_copy(h, k):
        place = out_ref.at[rows(h), cols(back(k) * 2 + x)]
        return remote(place, place, fs_sem.at[h, k], fr_sem.at[h, k], {"tp": partner})

    def f_arrival(h, k):
        place = out_ref.at[rows(h), cols(back(k) * 2 + other_x)]
        return remote(place, place, fs_sem.at[h, k], fr_sem.at[h, k], {"tp": partner})

    for k in range(nz):

        def to_partner(here, value, k=k):
            x_out[k, :, here] = value.astype(x_out.dtype)

        chunk(k, to_partner)
        x_copy(0, k).start()
    for h in range(1, HALVES):
        for k in range(nz):
            x_copy(h, k).start()
    for k in range(nz):

        def to_own(here, value, k=k):
            own[k, :, here] = value

        chunk(nz + k, to_own)

    def pair_sums(h):
        for k in range(nz):
            x_copy(h, k).wait_recv()
            value = own[k, rows(h), :] + x_in[k, rows(h), :].astype(jnp.float32)
            if k < nz - 1:
                z_out[k, rows(h), :] = value.astype(z_out.dtype)
                z_copy(h, k).start()
            else:
                own[k, rows(h), :] = value

    def finish(h):
        for k in range(nz - 1):
            z_copy(h, k).wait_recv()
        for b in range(part // BLK):
            here = slice(b * BLK, (b + 1) * BLK)
            value = own[nz - 1, rows(h), here]
            for k in range(nz - 1):
                value = value + z_in[k, rows(h), here].astype(jnp.float32)
            place = pl.ds(pl.multiple_of(me * part + b * BLK, BLK), BLK)
            scale = s2_ref[:, place]
            coded = jnp.minimum(jnp.maximum(value / scale, -SATURATION), SATURATION).astype(jnp.bfloat16)
            plain = jnp.dot(coded, signs, preferred_element_type=jnp.float32) * (scale * norm)
            out_ref[rows(h), place] = plain.astype(out_ref.dtype)
        for k in range(nz - 1):
            g_copy(h, k).start()
        f_copy(h, nz - 1).start()

    def forward(h):
        for k in range(nz - 1):
            g_arrival(h, k).wait_recv()
            f_copy(h, k).start()

    pair_sums(0)
    finish(0)
    for h in range(1, HALVES):
        pair_sums(h)
        forward(h - 1)
        finish(h)
    forward(HALVES - 1)
    for h in range(HALVES):
        for k in range(nz):
            f_arrival(h, k).wait_recv()
    for h in range(HALVES):
        for k in range(nz):
            x_copy(h, k).wait_send()
            f_copy(h, k).wait_send()
            if k < nz - 1:
                z_copy(h, k).wait_send()
                g_copy(h, k).wait_send()


def project(n_tp, o, stat, w, s1, s2, signs):
    tokens, width = o.shape
    columns = w.shape[1]
    nz = n_tp // 2
    part = columns // n_tp
    vmem = pl.BlockSpec(memory_space=pltpu.VMEM)
    sem = pltpu.SemaphoreType.DMA
    return pl.pallas_call(
        functools.partial(project_kernel, n_tp),
        out_shape=jax.ShapeDtypeStruct((tokens, columns), jnp.bfloat16),
        in_specs=[vmem, vmem, pl.BlockSpec(memory_space=pl.ANY), vmem, vmem, vmem],
        out_specs=vmem,
        scratch_shapes=[
            pltpu.VMEM((tokens, width), jnp.bfloat16),
            pltpu.VMEM((tokens, BLK), jnp.float32),
            pltpu.VMEM((tokens, width), jnp.bfloat16),
            pltpu.VMEM((SLOTS, width, part), jnp.bfloat16),
            pltpu.VMEM((nz, tokens, part), jnp.bfloat16),
            pltpu.VMEM((nz, tokens, part), jnp.bfloat16),
            pltpu.VMEM((nz, tokens, part), jnp.float32),
            pltpu.VMEM((nz - 1, tokens, part), jnp.bfloat16),
            pltpu.VMEM((nz - 1, tokens, part), jnp.bfloat16),
            sem((SLOTS,)),
            sem((2,)),
            sem((2,)),
        ]
        + [sem((HALVES, nz))] * 8,
        compiler_params=pltpu.CompilerParams(
            collective_id=0, has_side_effects=True, vmem_limit_bytes=56 * 2**20
        ),
    )(o, stat, w, s1, s2, signs)


def shards(n_tp, n_sub, queries, kv_cache, out_proj, first_scales, second_scales):
    o, stat = attention(n_sub, queries, kv_cache[0])
    own_scales = lax.dynamic_index_in_dim(first_scales, lax.axis_index("tp"), 0, keepdims=True)
    s1 = jnp.repeat(own_scales, BLK, axis=1)
    s2 = jnp.repeat(second_scales[None, :], BLK, axis=1)
    signs = jnp.asarray(hadamard_signs(), jnp.bfloat16)
    return project(n_tp, o, stat, out_proj, s1, s2, signs)


def solution(mesh):
    placed = (
        P("rep", "tp"),
        P("tp", ("rep", "sub"), None),
        P("tp", "sub"),
        P(None, "sub"),
        P("sub"),
    )
    return jax.shard_map(
        functools.partial(shards, mesh.shape["tp"], mesh.shape["sub"]),
        mesh=mesh,
        in_specs=placed,
        out_specs=P("rep", "sub"),
        check_vma=False,
    )
```
